32 devices in a mesh: ctx: 8 (over z, x), tp: 4 (over y, core).
Axes of the slice: x: 2, y: 2, z: 4, core: 2. Of those that a mesh axis runs over, the one named last changes fastest.
Arguments:
- queries: bfloat16 [8192, 4096], P(('ctx', 'tp')), may hold values from -40 to 40
- keys_in: bfloat16 [8192, 1024], P(('ctx', 'tp')), may hold values from -4 to 4
- values_in: bfloat16 [8192, 1024], P(('ctx', 'tp')), may hold values from -6 to 6
- grad_output: bfloat16 [8192, 4096], P(('ctx', 'tp')), may hold values from -6 to 6
- beacon_keys: bfloat16 [1024, 1024], P('ctx', 'tp'), may hold values from -6 to 6
- beacon_values: bfloat16 [1024, 1024], P('ctx', 'tp'), may hold values from -6 to 6
- read_blocks: int32 [8, 4], P('ctx'), may hold values from 0 to 6, as said below
- read_counts: int32 [8], P('ctx'), may hold values from 0 to 4, as said below
Outputs:
- attn_out: bfloat16 [8192, 4096], P(('ctx', 'tp'))
- grad_queries: bfloat16 [8192, 4096], P(('ctx', 'tp'))
- grad_keys: bfloat16 [8192, 1024], P(('ctx', 'tp'))
- grad_values: bfloat16 [8192, 1024], P(('ctx', 'tp'))
- grad_beacon_keys: bfloat16 [1024, 1024], P('ctx', 'tp')
- grad_beacon_values: bfloat16 [1024, 1024], P('ctx', 'tp')
The draws below stay inside these ranges and needn't reach their ends.
Inputs may be any that keep to these rules, and one draw needn't show every extreme that they name: `read_blocks`: row s lists distinct blocks of earlier segments in its first read_counts[s] slots, block s - 1 first; unused slots hold 0. The last segment reads block 3 in its second slot. read_counts[s] is at most min(s, 4); segment 0 reads nothing and the last segment uses all 4 slots.
All inputs are finite; a program needn't handle non-finite values.
Results may differ from the reference program's by a relative error of at most 0.01.
Values may be sent and summed in bfloat16 or wider, within the bound.
A program may use at most 128 MiB of HBM per device.

```python
import jax
import jax.numpy as jnp
from jax import lax

HQ = 32
KVH = 8
HD = 128
SEG = 1024
NREAD = 4
BEAC = 128
NSEG = 8
TOKENS = 8192


def query_key_pair(key):
    query_seed = jax.random.fold_in(key, 101)
    key_seed = jax.random.fold_in(key, 102)
    query_vals = jax.random.truncated_normal(query_seed, -4.0, 4.0, (TOKENS, HQ * HD), jnp.float32)
    key_vals = jax.random.truncated_normal(key_seed, -4.0, 4.0, (TOKENS, KVH * HD), jnp.float32)
    return (query_vals, key_vals)


def draw_queries(key, part):
    return query_key_pair(key)[0].astype(jnp.bfloat16)


def draw_keys_in(key, part):
    return query_key_pair(key)[1].astype(jnp.bfloat16)


def shuffle_one(subkey):
    return jax.random.permutation(subkey, NSEG).astype(jnp.int32)


def read_lists(key):
    base = jax.random.fold_in(key, 303)
    count_seed, order_seed = jax.random.split(base)
    segments = jnp.arange(NSEG, dtype=jnp.int32)
    ceiling = jnp.minimum(segments, NREAD)
    counts = jax.random.randint(count_seed, (NSEG,), 1, NREAD + 1).astype(jnp.int32)
    counts = jnp.minimum(counts, ceiling)
    counts = jnp.where(segments == NSEG - 1, NREAD, counts).astype(jnp.int32)
    shuffled = jax.vmap(shuffle_one)(jax.random.split(order_seed, NSEG))
    block_ids = segments[None, :]
    scores = jnp.where(block_ids < segments[:, None], shuffled + 2, NSEG + 2 + block_ids)
    forced = (segments[:, None] == NSEG - 1) & (block_ids == NSEG // 2 - 1)
    scores = jnp.where(forced, 1, scores)
    scores = jnp.where(block_ids == segments[:, None] - 1, 0, scores)
    ranking = jnp.argsort(scores, axis=1, stable=True).astype(jnp.int32)[:, :NREAD]
    slots = jnp.arange(NREAD, dtype=jnp.int32)[None, :]
    blocks = jnp.where(slots < counts[:, None], ranking, 0).astype(jnp.int32)
    return (blocks, counts)


def draw_read_blocks(key, part):
    return read_lists(key)[0]


def draw_read_counts(key, part):
    return read_lists(key)[1]


def shard_levels(key, shape, pieces, smallest, largest):
    def one(position, blocks):
        draws = jax.random.uniform(jax.random.fold_in(jax.random.fold_in(key, 6), position), (blocks,), jnp.float32, smallest / len(pieces), largest / len(pieces))
        return jnp.repeat(jnp.exp(draws), shape[position] // blocks).reshape((-1,) + (1,) * (len(shape) - position - 1))

    factor_of = one(*pieces[0])
    for cut in pieces[1:]:
        factor_of = factor_of * one(*cut)
    return factor_of


def gaussian(rng, shape, spread, limit, cuts=(), kind=jnp.bfloat16):
    gain = shard_levels(rng, shape, cuts, -0.22, 0.18) if cuts else 1.0
    drawn = jax.random.normal(rng, shape, jnp.float32) * spread * gain
    return jnp.minimum(jnp.maximum(drawn, -limit), limit).astype(kind)


def setup_inputs(seed: int = 0) -> dict:
    streams_of = jax.random.split(jax.random.key(seed), 9)
    queries = draw_queries(jax.random.fold_in(streams_of[8], 71), 0)
    keys_in = draw_keys_in(jax.random.fold_in(streams_of[8], 71), 0)
    values_in = gaussian(streams_of[2], (TOKENS, KVH * HD), 1.0, 6.0, ((0, 32),))
    grad_output = gaussian(streams_of[3], (TOKENS, HQ * HD), 1.0, 6.0, ((0, 32),))
    beacon_keys = gaussian(streams_of[4], (NSEG * BEAC, KVH * HD), 1.0, 6.0, ((0, 8), (1, 4)))
    beacon_values = gaussian(streams_of[5], (NSEG * BEAC, KVH * HD), 1.0, 6.0, ((0, 8), (1, 4)))
    read_blocks = draw_read_blocks(jax.random.fold_in(streams_of[8], 71), 0)
    read_counts = draw_read_counts(jax.random.fold_in(streams_of[8], 71), 0)
    return {"queries": queries, "keys_in": keys_in, "values_in": values_in, "grad_output": grad_output, "beacon_keys": beacon_keys, "beacon_values": beacon_values, "read_blocks": read_blocks, "read_counts": read_counts}


def head_grads(query_rows, key_rows, value_rows, grad_rows, allowed, score_scale):
    scores = jnp.dot(query_rows, key_rows.T, preferred_element_type=jnp.float32) * score_scale
    scores = jnp.where(allowed, scores, -1e30)
    row_max = jnp.max(scores, axis=1, keepdims=True)
    weights = jnp.exp(scores - row_max)
    prob_full = weights / jnp.sum(weights, axis=1, keepdims=True)
    prob_half = prob_full.astype(jnp.bfloat16)
    output = jnp.dot(prob_half, value_rows, preferred_element_type=jnp.float32).astype(jnp.bfloat16)
    grad_prob = jnp.dot(grad_rows, value_rows.T, preferred_element_type=jnp.float32)
    row_delta = jnp.sum(grad_rows.astype(jnp.float32) * output.astype(jnp.float32), axis=1, keepdims=True)
    dscores = (prob_full * (grad_prob - row_delta) * score_scale).astype(jnp.bfloat16)
    grad_query = jnp.dot(dscores, key_rows, preferred_element_type=jnp.float32).astype(jnp.bfloat16)
    grad_key = jnp.dot(dscores.T, query_rows, preferred_element_type=jnp.float32)
    grad_value = jnp.dot(prob_half.T, grad_rows, preferred_element_type=jnp.float32)
    return output, grad_query, grad_key, grad_value


def reference(queries, keys_in, values_in, grad_output, beacon_keys, beacon_values, read_blocks, read_counts):
    score_scale = HD ** -0.5
    group_size = HQ // KVH
    beacon_rows = NREAD * BEAC
    col_width = KVH * HD
    positions = jnp.arange(SEG, dtype=jnp.int32)
    causal = positions[None, :] <= positions[:, None]
    blocks_k = beacon_keys.reshape(NSEG, BEAC, col_width)
    blocks_v = beacon_values.reshape(NSEG, BEAC, col_width)

    def segment(totals, inputs):
        dense_k, dense_v = totals
        seg_q, seg_k, seg_v, seg_g, read_row, read_count = inputs
        slot_ok = jnp.arange(NREAD, dtype=jnp.int32) < read_count
        valid_keys = jnp.repeat(slot_ok, BEAC)
        allowed = jnp.concatenate([causal, jnp.broadcast_to(valid_keys[None, :], (SEG, beacon_rows))], axis=1)
        chosen_k = jnp.take(blocks_k, read_row, axis=0).reshape(beacon_rows, col_width)
        chosen_v = jnp.take(blocks_v, read_row, axis=0).reshape(beacon_rows, col_width)
        query_heads = seg_q.reshape(SEG, HQ, HD).transpose(1, 0, 2)
        grad_heads = seg_g.reshape(SEG, HQ, HD).transpose(1, 0, 2)
        key_heads = jnp.concatenate([seg_k, chosen_k], axis=0).reshape(SEG + beacon_rows, KVH, HD).transpose(1, 0, 2)
        value_heads = jnp.concatenate([seg_v, chosen_v], axis=0).reshape(SEG + beacon_rows, KVH, HD).transpose(1, 0, 2)

        def per_head(head_index):
            shared = head_index // group_size
            return head_grads(query_heads[head_index], key_heads[shared], value_heads[shared], grad_heads[head_index], allowed, score_scale)

        outputs, grad_query, grad_key, grad_value = lax.map(per_head, jnp.arange(HQ, dtype=jnp.int32))
        grad_key = jnp.sum(grad_key.reshape(KVH, group_size, SEG + beacon_rows, HD), axis=1)
        grad_value = jnp.sum(grad_value.reshape(KVH, group_size, SEG + beacon_rows, HD), axis=1)
        local_k = grad_key[:, :SEG].transpose(1, 0, 2).reshape(SEG, col_width).astype(jnp.bfloat16)
        local_v = grad_value[:, :SEG].transpose(1, 0, 2).reshape(SEG, col_width).astype(jnp.bfloat16)
        slot_mask = slot_ok.astype(jnp.float32)[:, None, None]
        part_k = grad_key[:, SEG:].transpose(1, 0, 2).reshape(NREAD, BEAC, col_width) * slot_mask
        part_v = grad_value[:, SEG:].transpose(1, 0, 2).reshape(NREAD, BEAC, col_width) * slot_mask
        dense_k = dense_k.at[read_row].add(part_k)
        dense_v = dense_v.at[read_row].add(part_v)
        seg_out = outputs.transpose(1, 0, 2).reshape(SEG, HQ * HD)
        seg_gq = grad_query.transpose(1, 0, 2).reshape(SEG, HQ * HD)
        return (dense_k, dense_v), (seg_out, seg_gq, local_k, local_v)

    start = (jnp.zeros((NSEG, BEAC, col_width), jnp.float32), jnp.zeros((NSEG, BEAC, col_width), jnp.float32))
    inputs = (queries.reshape(NSEG, SEG, HQ * HD), keys_in.reshape(NSEG, SEG, col_width),
              values_in.reshape(NSEG, SEG, col_width), grad_output.reshape(NSEG, SEG, HQ * HD),
              read_blocks, read_counts)
    (dense_k, dense_v), (all_out, all_gq, all_gk, all_gv) = lax.scan(segment, start, inputs)
    return (all_out.reshape(TOKENS, HQ * HD), all_gq.reshape(TOKENS, HQ * HD),
            all_gk.reshape(TOKENS, col_width), all_gv.reshape(TOKENS, col_width),
            dense_k.reshape(NSEG * BEAC, col_width).astype(jnp.bfloat16),
            dense_v.reshape(NSEG * BEAC, col_width).astype(jnp.bfloat16))
```

```python
import functools
import math

import jax
import jax.numpy as jnp
from jax import lax
from jax.experimental import pallas as pl
from jax.experimental.pallas import tpu as pltpu
from jax.sharding import PartitionSpec as P

HD = 128
CORES = 2
BF = jnp.bfloat16
F32 = jnp.float32


def nt(a, b):
    return lax.dot_general(a, b, (((1,), (1,)), ((), ())), preferred_element_type=F32)


def nn(a, b):
    return jnp.dot(a, b, preferred_element_type=F32)


def attention_kernel(
    group, prev_groups, slots, half,
    count_ref, hi_ref,
    q_ref, g_ref, k_ref, v_ref, kp_ref, vp_ref, kb_ref, vb_ref,
    out_ref, gq_ref, dko_ref, dvo_ref, dkp_ref, dvp_ref, dkb_ref, dvb_ref,
    acc_k, acc_v,
):
    step = pl.program_id(1)
    rows = q_ref.shape[0]
    own = k_ref.shape[0]
    prev = kp_ref.shape[0]
    beac = kb_ref.shape[0]
    chunk = prev // prev_groups
    block = beac // slots
    scale = HD ** (-0.5)
    c = scale * math.log2(math.e)
    q = q_ref[...]
    g = g_ref[...]
    hi = hi_ref[0]
    count = count_ref[0]

    diag = lax.broadcasted_iota(jnp.int32, (half, half), 0) <= lax.broadcasted_iota(
        jnp.int32, (half, half), 1
    )
    pieces = []
    for i in range(0, own, half):
        pieces.append((i, i, k_ref[i : i + half, :], v_ref[i : i + half, :], None))
    for d in range(prev_groups):
        at = d * chunk
        pieces.append(
            (own + at, 0, kp_ref[at : at + chunk, :], vp_ref[at : at + chunk, :], hi > d)
        )
    for j in range(slots):
        at = j * block
        pieces.append(
            (own + prev + at, 0, kb_ref[at : at + block, :], vb_ref[at : at + block, :], count > j)
        )

    def pad_rows(x, start, fill):
        if start == 0:
            return x
        return jnp.concatenate([jnp.full((x.shape[0], start), fill, x.dtype), x], axis=1)

    scores = []
    row_max = None
    for _, start, keys, _, ok in pieces:
        s = nt(keys, q[start:, :])
        if ok is None:
            d = jnp.where(diag, s[:, :half], -1e30)
            s = d if s.shape[1] == half else jnp.concatenate([d, s[:, half:]], axis=1)
            top = jnp.max(s, axis=0, keepdims=True)
        else:
            top = jnp.max(s, axis=0, keepdims=True) + jnp.where(ok, 0.0, -1e30)
        top = pad_rows(top, start, -1e30)
        row_max = top if row_max is None else jnp.maximum(row_max, top)
        scores.append(s)
    shift = row_max * c
    weights = []
    total = None
    for (_, start, _, _, ok), s in zip(pieces, scores):
        m = shift[:, start:]
        if ok is not None:
            m = m + jnp.where(ok, 0.0, 1e30)
        w = jnp.exp2(s * c - m)
        part = pad_rows(jnp.sum(w, axis=0, keepdims=True), start, 0.0)
        total = part if total is None else total + part
        weights.append(w)
    inv = 1.0 / total
    out_t = None
    probs = []
    for (_, start, _, vals, _), w in zip(pieces, weights):
        p = (w * inv[:, start:]).astype(BF)
        probs.append(p)
        o = pad_rows(nn(vals.T, p), start, 0.0)
        out_t = o if out_t is None else out_t + o
    out = out_t.T.astype(BF)
    out_ref[...] = out
    delta = jnp.sum(out.astype(F32) * g.astype(F32), axis=1, keepdims=True).T
    r2 = inv * scale

    @pl.when(step == 0)
    def _():
        acc_k[...] = jnp.zeros_like(acc_k)
        acc_v[...] = jnp.zeros_like(acc_v)

    gq_t = None
    for (at, start, keys, vals, _), w, p in zip(pieces, weights, probs):
        n = keys.shape[0]
        dp = nt(vals, g[start:, :])
        ds = ((w * r2[:, start:]) * (dp - delta[:, start:])).astype(BF)
        acc_v[at : at + n, :] += nn(p, g[start:, :])
        acc_k[at : at + n, :] += nn(ds, q[start:, :])
        d = pad_rows(nn(keys.T, ds), start, 0.0)
        gq_t = d if gq_t is None else gq_t + d
    gq_ref[...] = gq_t.T.astype(BF)

    @pl.when(step == group - 1)
    def _():
        dko_ref[...] = acc_k[:own, :]
        dvo_ref[...] = acc_v[:own, :]
        dkp_ref[...] = acc_k[own : own + prev, :].astype(BF)
        dvp_ref[...] = acc_v[own : own + prev, :].astype(BF)
        dkb_ref[...] = acc_k[own + prev :, :].astype(BF)
        dvb_ref[...] = acc_v[own + prev :, :].astype(BF)


def attention(q, g, k, v, kp, vp, kb, vb, count, hi, prev_groups, slots):
    rows, q_cols = q.shape
    own, kv_cols = k.shape
    prev, beac = kp.shape[0], kb.shape[0]
    heads, kv_heads = q_cols // HD, kv_cols // HD
    group = heads // kv_heads
    half = own // 2
    per_q = pl.BlockSpec((rows, HD), lambda a, b, *_: (0, a * group + b))

    def per_kv(n):
        return pl.BlockSpec((n, HD), lambda a, b, *_: (0, a))

    keys = own + prev + beac
    return pl.pallas_call(
        functools.partial(attention_kernel, group, prev_groups, slots, half),
        grid_spec=pltpu.PrefetchScalarGridSpec(
            num_scalar_prefetch=2,
            grid=(kv_heads, group),
            in_specs=[per_q, per_q, per_kv(own), per_kv(own), per_kv(prev), per_kv(prev), per_kv(beac), per_kv(beac)],
            out_specs=[per_q, per_q, per_kv(own), per_kv(own), per_kv(prev), per_kv(prev), per_kv(beac), per_kv(beac)],
            scratch_shapes=[pltpu.VMEM((keys, HD), F32), pltpu.VMEM((keys, HD), F32)],
        ),
        out_shape=[
            jax.ShapeDtypeStruct(q.shape, BF),
            jax.ShapeDtypeStruct(q.shape, BF),
            jax.ShapeDtypeStruct(k.shape, F32),
            jax.ShapeDtypeStruct(k.shape, F32),
            jax.ShapeDtypeStruct(kp.shape, BF),
            jax.ShapeDtypeStruct(kp.shape, BF),
            jax.ShapeDtypeStruct(kb.shape, BF),
            jax.ShapeDtypeStruct(kb.shape, BF),
        ],
        compiler_params=pltpu.CompilerParams(vmem_limit_bytes=50 * 1024 * 1024),
        cost_estimate=pl.CostEstimate(
            flops=12 * heads * rows * keys * HD, bytes_accessed=4 * q.size * 2, transcendentals=heads * rows * keys
        ),
    )(count, hi, q, g, k, v, kp, vp, kb, vb)


def shards(
    queries, keys_in, values_in, grad_output, beacon_keys, beacon_values, read_blocks, read_counts
):
    tp = lax.axis_size("tp")
    owners = lax.axis_size("ctx")
    groups = tp // CORES
    t = lax.axis_index("tp")
    hi, lo = t // CORES, t % CORES
    tokens = queries.shape[0]
    block_rows, bw = beacon_keys.shape
    slots = read_blocks.shape[1]
    row, count = read_blocks[0], read_counts[0]

    def column_half(x, which):
        w = x.shape[1] // tp
        parts = [
            lax.dynamic_slice_in_dim(x, (CORES * j + which) * w, w, axis=1) for j in range(groups)
        ]
        return jnp.concatenate(parts, axis=1)

    sibling = [(i, i ^ 1) for i in range(tp)]

    def by_rank(mine, theirs, axis):
        first = jnp.where(lo == 0, mine, theirs)
        second = jnp.where(lo == 0, theirs, mine)
        return jnp.concatenate([first, second], axis=axis)

    def swap_in(*arrays):
        widths = [a.shape[1] // CORES for a in arrays]
        send = jnp.concatenate([column_half(a, 1 - lo) for a in arrays], axis=1)
        got = lax.ppermute(send, "tp", sibling)
        res, at = [], 0
        for a, w in zip(arrays, widths):
            res.append(by_rank(column_half(a, lo), got[:, at : at + w], 0))
            at += w
        return res

    all_b = lax.all_gather(
        jnp.concatenate([beacon_keys, beacon_values], axis=1), "ctx", axis=0, tiled=True
    )
    k, v = swap_in(keys_in, values_in)
    kv = jnp.concatenate([k, v], axis=1)
    prevs = []
    for d in range(1, groups):
        pairs = [(i, i + CORES * d) for i in range(tp - CORES * d)]
        prevs.append(lax.ppermute(kv, "tp", pairs))
    kvp = jnp.concatenate(prevs, axis=0)
    half_cols = k.shape[1]
    q, g = swap_in(queries, grad_output)

    mine = jnp.concatenate(
        [lax.dynamic_slice_in_dim(all_b, row[j] * block_rows, block_rows, axis=0) for j in range(slots)],
        axis=0,
    )
    quarters = [mine]
    for d in range(1, groups):
        pairs = [(i, (i + CORES * d) % tp) for i in range(tp)]
        quarters.append(lax.ppermute(mine, "tp", pairs))
    def ordered(lo_col, hi_col):
        res = []
        for j in range(groups):
            x = quarters[0][:, lo_col:hi_col]
            for d in range(1, groups):
                x = jnp.where((hi - d) % groups == j, quarters[d][:, lo_col:hi_col], x)
            res.append(x)
        return jnp.concatenate(res, axis=1)

    kb, vb = ordered(0, bw), ordered(bw, 2 * bw)

    out, gq, dko, dvo, dkp, dvp, dkb, dvb = attention(
        q, g, k, v, kvp[:, :half_cols], kvp[:, half_cols:], kb, vb,
        count[None], hi[None].astype(jnp.int32), groups - 1, slots,
    )

    def quarter(x, j):
        return lax.dynamic_slice_in_dim(x, j * bw, bw, axis=1)

    def both(j):
        return jnp.concatenate([quarter(dkb, j), quarter(dvb, j)], axis=1)

    beacon = both(hi).astype(F32)
    for d in range(1, groups):
        pairs = [(i, (i + CORES * d) % tp) for i in range(tp)]
        beacon = beacon + lax.ppermute(both((hi + d) % groups), "tp", pairs).astype(F32)
    beacon = beacon.reshape(slots, block_rows, 2 * bw)
    used = jnp.arange(slots, dtype=jnp.int32) < count
    ids = jnp.arange(owners, dtype=jnp.int32)
    dense = jnp.zeros((owners, block_rows, 2 * bw), F32)
    for j in range(slots):
        hit = (ids == row[j]) & used[j]
        dense = dense + jnp.where(hit[:, None, None], beacon[j][None], 0.0)
    dense = dense.astype(BF).reshape(owners * block_rows, 2 * bw)
    own_b = lax.psum_scatter(dense, "ctx", scatter_dimension=0, tiled=True)

    rows_g = k.shape[0]
    kvg = jnp.concatenate([dko, dvo], axis=1)
    back = jnp.concatenate([dkp, dvp], axis=1)
    for d in range(1, groups):
        pairs = [(i + CORES * d, i) for i in range(tp - CORES * d)]
        kvg = kvg + lax.ppermute(back[(d - 1) * rows_g : d * rows_g], "tp", pairs).astype(F32)
    kvg = kvg.astype(BF)

    def swap_out(*arrays):
        send = jnp.concatenate(
            [lax.dynamic_slice_in_dim(a, (1 - lo) * tokens, tokens, axis=0) for a in arrays], axis=1
        )
        got = lax.ppermute(send, "tp", sibling)
        res, at = [], 0
        for a in arrays:
            n = a.shape[1]
            keep = lax.dynamic_slice_in_dim(a, lo * tokens, tokens, axis=0)
            new = got[:, at : at + n]
            at += n
            w = n // groups
            cols = []
            for j in range(groups):
                cols.append(by_rank(keep[:, j * w : (j + 1) * w], new[:, j * w : (j + 1) * w], 1))
            res.append(jnp.concatenate(cols, axis=1))
        return res

    tok_out, tok_gq = swap_out(out, gq)
    tok_gk, tok_gv = swap_out(kvg[:, :half_cols], kvg[:, half_cols:])
    return (tok_out, tok_gq, tok_gk, tok_gv, own_b[:, :bw], own_b[:, bw:])


def solution(mesh):
    tok = P(("ctx", "tp"), None)
    bea = P("ctx", "tp")
    return jax.shard_map(
        shards,
        mesh=mesh,
        in_specs=(tok, tok, tok, tok, bea, bea, P("ctx", None), P("ctx")),
        out_specs=(tok, tok, tok, tok, bea, bea),
        check_vma=False,
    )
```

```python
import functools
import math

import jax
import jax.numpy as jnp
from jax import lax
from jax.experimental import pallas as pl
from jax.experimental.pallas import tpu as pltpu
from jax.sharding import PartitionSpec as P

HD = 128
CORES = 2
BF = jnp.bfloat16
F32 = jnp.float32


def nt(a, b):
    return lax.dot_general(a, b, (((1,), (1,)), ((), ())), preferred_element_type=F32)


def nn(a, b):
    return jnp.dot(a, b, preferred_element_type=F32)


def attention_kernel(
    group, prev_groups, slots, half,
    count_ref, hi_ref,
    q_ref, g_ref, k_ref, v_ref, kp_ref, vp_ref, kb_ref, vb_ref,
    out_ref, gq_ref, dko_ref, dvo_ref, dkp_ref, dvp_ref, dkb_ref, dvb_ref,
    acc_k, acc_v,
):
    step = pl.program_id(1)
    rows = q_ref.shape[0]
    own = k_ref.shape[0]
    prev = kp_ref.shape[0]
    beac = kb_ref.shape[0]
    chunk = prev // prev_groups
    block = beac // slots
    scale = HD ** (-0.5)
    c = scale * math.log2(math.e)
    q = q_ref[...]
    g = g_ref[...]
    hi = hi_ref[0]
    count = count_ref[0]

    diag = lax.broadcasted_iota(jnp.int32, (half, half), 0) <= lax.broadcasted_iota(
        jnp.int32, (half, half), 1
    )
    pieces = []
    for i in range(0, own, half):
        pieces.append((i, i, k_ref[i : i + half, :], v_ref[i : i + half, :], None))
    for d in range(prev_groups):
        at = d * chunk
        pieces.append(
            (own + at, 0, kp_ref[at : at + chunk, :], vp_ref[at : at + chunk, :], hi > d)
        )
    for j in range(slots):
        at = j * block
        pieces.append(
            (own + prev + at, 0, kb_ref[at : at + block, :], vb_ref[at : at + block, :], count > j)
        )

    def pad_rows(x, start, fill):
        if start == 0:
            return x
        return jnp.concatenate([jnp.full((x.shape[0], start), fill, x.dtype), x], axis=1)

    scores = []
    row_max = None
    for _, start, keys, _, ok in pieces:
        s = nt(keys, q[start:, :])
        if ok is None:
            d = jnp.where(diag, s[:, :half], -1e30)
            s = d if s.shape[1] == half else jnp.concatenate([d, s[:, half:]], axis=1)
            top = jnp.max(s, axis=0, keepdims=True)
        else:
            top = jnp.max(s, axis=0, keepdims=True) + jnp.where(ok, 0.0, -1e30)
        top = pad_rows(top, start, -1e30)
        row_max = top if row_max is None else jnp.maximum(row_max, top)
        scores.append(s)
    shift = row_max * c
    weights = []
    total = None
    for (_, start, _, _, ok), s in zip(pieces, scores):
        m = shift[:, start:]
        if ok is not None:
            m = m + jnp.where(ok, 0.0, 1e30)
        w = jnp.exp2(s * c - m)
        part = pad_rows(jnp.sum(w, axis=0, keepdims=True), start, 0.0)
        total = part if total is None else total + part
        weights.append(w)
    inv = 1.0 / total
    out_t = None
    probs = []
    for (_, start, _, vals, _), w in zip(pieces, weights):
        p = (w * inv[:, start:]).astype(BF)
        probs.append(p)
        o = pad_rows(nn(vals.T, p), start, 0.0)
        out_t = o if out_t is None else out_t + o
    out = out_t.T.astype(BF)
    out_ref[...] = out
    delta = jnp.sum(out.astype(F32) * g.astype(F32), axis=1, keepdims=True).T
    r2 = inv * scale

    @pl.when(step == 0)
    def _():
        acc_k[...] = jnp.zeros_like(acc_k)
        acc_v[...] = jnp.zeros_like(acc_v)

    gq_t = None
    for (at, start, keys, vals, _), w, p in zip(pieces, weights, probs):
        n = keys.shape[0]
        dp = nt(vals, g[start:, :])
        ds = ((w * r2[:, start:]) * (dp - delta[:, start:])).astype(BF)
        acc_v[at : at + n, :] += nn(p, g[start:, :])
        acc_k[at : at + n, :] += nn(ds, q[start:, :])
        d = pad_rows(nn(keys.T, ds), start, 0.0)
        gq_t = d if gq_t is None else gq_t + d
    gq_ref[...] = gq_t.T.astype(BF)

    @pl.when(step == group - 1)
    def _():
        dko_ref[...] = acc_k[:own, :]
        dvo_ref[...] = acc_v[:own, :]
        dkp_ref[...] = acc_k[own : own + prev, :].astype(BF)
        dvp_ref[...] = acc_v[own : own + prev, :].astype(BF)
        dkb_ref[...] = acc_k[own + prev :, :].astype(BF)
        dvb_ref[...] = acc_v[own + prev :, :].astype(BF)


def attention(q, g, k, v, kp, vp, kb, vb, count, hi, prev_groups, slots):
    rows, q_cols = q.shape
    own, kv_cols = k.shape
    prev, beac = kp.shape[0], kb.shape[0]
    heads, kv_heads = q_cols // HD, kv_cols // HD
    group = heads // kv_heads
    half = own // 2
    per_q = pl.BlockSpec((rows, HD), lambda a, b, *_: (0, a * group + b))

    def per_kv(n):
        return pl.BlockSpec((n, HD), lambda a, b, *_: (0, a))

    keys = own + prev + beac
    return pl.pallas_call(
        functools.partial(attention_kernel, group, prev_groups, slots, half),
        grid_spec=pltpu.PrefetchScalarGridSpec(
            num_scalar_prefetch=2,
            grid=(kv_heads, group),
            in_specs=[per_q, per_q, per_kv(own), per_kv(own), per_kv(prev), per_kv(prev), per_kv(beac), per_kv(beac)],
            out_specs=[per_q, per_q, per_kv(own), per_kv(own), per_kv(prev), per_kv(prev), per_kv(beac), per_kv(beac)],
            scratch_shapes=[pltpu.VMEM((keys, HD), F32), pltpu.VMEM((keys, HD), F32)],
        ),
        out_shape=[
            jax.ShapeDtypeStruct(q.shape, BF),
            jax.ShapeDtypeStruct(q.shape, BF),
            jax.ShapeDtypeStruct(k.shape, F32),
            jax.ShapeDtypeStruct(k.shape, F32),
            jax.ShapeDtypeStruct(kp.shape, BF),
            jax.ShapeDtypeStruct(kp.shape, BF),
            jax.ShapeDtypeStruct(kb.shape, BF),
            jax.ShapeDtypeStruct(kb.shape, BF),
        ],
        compiler_params=pltpu.CompilerParams(vmem_limit_bytes=50 * 1024 * 1024),
        cost_estimate=pl.CostEstimate(
            flops=12 * heads * rows * keys * HD, bytes_accessed=4 * q.size * 2, transcendentals=heads * rows * keys
        ),
    )(count, hi, q, g, k, v, kp, vp, kb, vb)


def owners_kernel(dense_ref, out_ref, got, total, send_sem, recv_sem):
    me = lax.axis_index("ctx")
    n = got.shape[0]
    block = got.shape[1]
    barrier = pltpu.get_barrier_semaphore()
    for d in range(1, n):
        pl.semaphore_signal(
            barrier, inc=1, device_id={"ctx": lax.rem(me + d, n)}, device_id_type=pl.DeviceIdType.MESH
        )
    pl.semaphore_wait(barrier, n - 1)

    def copy(d):
        to = jnp.maximum(me - d, 0)
        return pltpu.make_async_remote_copy(
            src_ref=dense_ref.at[pl.ds(pl.multiple_of(to * block, block), block)],
            dst_ref=got.at[d],
            send_sem=send_sem.at[d],
            recv_sem=recv_sem.at[d],
            device_id={"ctx": to},
            device_id_type=pl.DeviceIdType.MESH,
        )

    for d in range(n - 1, 0, -1):

        @pl.when(me >= d)
        def _(d=d):
            copy(d).start()

    total[...] = jnp.zeros_like(total)
    for d in range(1, n):

        @pl.when(me + d < n)
        def _(d=d):
            copy(d).wait_recv()
            total[...] += got[d].astype(F32)

    out_ref[...] = total[...].astype(BF)
    for d in range(1, n):

        @pl.when(me >= d)
        def _(d=d):
            copy(d).wait_send()


def to_owners(dense, owners):
    block, width = dense.shape[0] // owners, dense.shape[1]
    return pl.pallas_call(
        owners_kernel,
        out_shape=jax.ShapeDtypeStruct((block, width), BF),
        in_specs=[pl.BlockSpec(memory_space=pltpu.VMEM)],
        out_specs=pl.BlockSpec(memory_space=pltpu.VMEM),
        scratch_shapes=[
            pltpu.VMEM((owners, block, width), BF),
            pltpu.VMEM((block, width), F32),
            pltpu.SemaphoreType.DMA((owners,)),
            pltpu.SemaphoreType.DMA((owners,)),
        ],
        compiler_params=pltpu.CompilerParams(
            collective_id=1, has_side_effects=True, vmem_limit_bytes=32 * 1024 * 1024
        ),
    )(dense)


def shards(
    queries, keys_in, values_in, grad_output, beacon_keys, beacon_values, read_blocks, read_counts
):
    tp = lax.axis_size("tp")
    owners = lax.axis_size("ctx")
    groups = tp // CORES
    t = lax.axis_index("tp")
    hi, lo = t // CORES, t % CORES
    tokens = queries.shape[0]
    block_rows, bw = beacon_keys.shape
    slots = read_blocks.shape[1]
    row, count = read_blocks[0], read_counts[0]

    def column_half(x, which):
        w = x.shape[1] // tp
        parts = [
            lax.dynamic_slice_in_dim(x, (CORES * j + which) * w, w, axis=1) for j in range(groups)
        ]
        return jnp.concatenate(parts, axis=1)

    sibling = [(i, i ^ 1) for i in range(tp)]

    def by_rank(mine, theirs, axis):
        first = jnp.where(lo == 0, mine, theirs)
        second = jnp.where(lo == 0, theirs, mine)
        return jnp.concatenate([first, second], axis=axis)

    def swap_in(*arrays):
        widths = [a.shape[1] // CORES for a in arrays]
        send = jnp.concatenate([column_half(a, 1 - lo) for a in arrays], axis=1)
        got = lax.ppermute(send, "tp", sibling)
        res, at = [], 0
        for a, w in zip(arrays, widths):
            res.append(by_rank(column_half(a, lo), got[:, at : at + w], 0))
            at += w
        return res

    all_b = lax.all_gather(
        jnp.concatenate([beacon_keys, beacon_values], axis=1), "ctx", axis=0, tiled=True
    )
    k, v = swap_in(keys_in, values_in)
    kv = jnp.concatenate([k, v], axis=1)
    prevs = []
    for d in range(1, groups):
        pairs = [(i, i + CORES * d) for i in range(tp - CORES * d)]
        prevs.append(lax.ppermute(kv, "tp", pairs))
    kvp = jnp.concatenate(prevs, axis=0)
    half_cols = k.shape[1]
    q, g = swap_in(queries, grad_output)

    mine = jnp.concatenate(
        [lax.dynamic_slice_in_dim(all_b, row[j] * block_rows, block_rows, axis=0) for j in range(slots)],
        axis=0,
    )
    quarters = [mine]
    for d in range(1, groups):
        pairs = [(i, (i + CORES * d) % tp) for i in range(tp)]
        quarters.append(lax.ppermute(mine, "tp", pairs))
    def ordered(lo_col, hi_col):
        res = []
        for j in range(groups):
            x = quarters[0][:, lo_col:hi_col]
            for d in range(1, groups):
                x = jnp.where((hi - d) % groups == j, quarters[d][:, lo_col:hi_col], x)
            res.append(x)
        return jnp.concatenate(res, axis=1)

    kb, vb = ordered(0, bw), ordered(bw, 2 * bw)

    out, gq, dko, dvo, dkp, dvp, dkb, dvb = attention(
        q, g, k, v, kvp[:, :half_cols], kvp[:, half_cols:], kb, vb,
        count[None], hi[None].astype(jnp.int32), groups - 1, slots,
    )

    def quarter(x, j):
        return lax.dynamic_slice_in_dim(x, j * bw, bw, axis=1)

    def both(j):
        return jnp.concatenate([quarter(dkb, j), quarter(dvb, j)], axis=1)

    beacon = both(hi).astype(F32)
    for d in range(1, groups):
        pairs = [(i, (i + CORES * d) % tp) for i in range(tp)]
        beacon = beacon + lax.ppermute(both((hi + d) % groups), "tp", pairs).astype(F32)
    beacon = beacon.reshape(slots, block_rows, 2 * bw)
    used = jnp.arange(slots, dtype=jnp.int32) < count
    ids = jnp.arange(owners, dtype=jnp.int32)
    dense = jnp.zeros((owners, block_rows, 2 * bw), F32)
    for j in range(slots):
        hit = (ids == row[j]) & used[j]
        dense = dense + jnp.where(hit[:, None, None], beacon[j][None], 0.0)
    dense = dense.astype(BF).reshape(owners * block_rows, 2 * bw)
    own_b = to_owners(dense, owners)

    rows_g = k.shape[0]
    kvg = jnp.concatenate([dko, dvo], axis=1)
    back = jnp.concatenate([dkp, dvp], axis=1)
    for d in range(1, groups):
        pairs = [(i + CORES * d, i) for i in range(tp - CORES * d)]
        kvg = kvg + lax.ppermute(back[(d - 1) * rows_g : d * rows_g], "tp", pairs).astype(F32)
    kvg = kvg.astype(BF)

    def swap_out(*arrays):
        send = jnp.concatenate(
            [lax.dynamic_slice_in_dim(a, (1 - lo) * tokens, tokens, axis=0) for a in arrays], axis=1
        )
        got = lax.ppermute(send, "tp", sibling)
        res, at = [], 0
        for a in arrays:
            n = a.shape[1]
            keep = lax.dynamic_slice_in_dim(a, lo * tokens, tokens, axis=0)
            new = got[:, at : at + n]
            at += n
            w = n // groups
            cols = []
            for j in range(groups):
                cols.append(by_rank(keep[:, j * w : (j + 1) * w], new[:, j * w : (j + 1) * w], 1))
            res.append(jnp.concatenate(cols, axis=1))
        return res

    tok_out, tok_gq = swap_out(out, gq)
    tok_gk, tok_gv = swap_out(kvg[:, :half_cols], kvg[:, half_cols:])
    return (tok_out, tok_gq, tok_gk, tok_gv, own_b[:, :bw], own_b[:, bw:])


def solution(mesh):
    tok = P(("ctx", "tp"), None)
    bea = P("ctx", "tp")
    return jax.shard_map(
        shards,
        mesh=mesh,
        in_specs=(tok, tok, tok, tok, bea, bea, P("ctx", None), P("ctx")),
        out_specs=(tok, tok, tok, tok, bea, bea),
        check_vma=False,
    )
```

```python
import functools
import math

import jax
import jax.numpy as jnp
from jax import lax
from jax.experimental import pallas as pl
from jax.experimental.pallas import tpu as pltpu
from jax.sharding import PartitionSpec as P

HD = 128
CORES = 2
BF = jnp.bfloat16
F32 = jnp.float32


def nt(a, b):
    return lax.dot_general(a, b, (((1,), (1,)), ((), ())), preferred_element_type=F32)


def nn(a, b):
    return jnp.dot(a, b, preferred_element_type=F32)


def attention_kernel(
    group, prev_groups, slots, half,
    count_ref, hi_ref,
    q_ref, g_ref, k_ref, v_ref, kp_ref, vp_ref, kb_ref, vb_ref,
    out_ref, gq_ref, dko_ref, dvo_ref, dkp_ref, dvp_ref, dkb_ref, dvb_ref,
    acc_k, acc_v,
):
    step = pl.program_id(1)
    rows = q_ref.shape[0]
    own = k_ref.shape[0]
    prev = kp_ref.shape[0]
    beac = kb_ref.shape[0]
    chunk = prev // prev_groups
    block = beac // slots
    scale = HD ** (-0.5)
    c = scale * math.log2(math.e)
    q = q_ref[...]
    g = g_ref[...]
    hi = hi_ref[0]
    count = count_ref[0]

    diag = lax.broadcasted_iota(jnp.int32, (half, half), 0) <= lax.broadcasted_iota(
        jnp.int32, (half, half), 1
    )
    pieces = []
    for i in range(0, own, half):
        pieces.append((i, i, k_ref[i : i + half, :], v_ref[i : i + half, :], None))
    for d in range(prev_groups):
        at = d * chunk
        pieces.append(
            (own + at, 0, kp_ref[at : at + chunk, :], vp_ref[at : at + chunk, :], hi > d)
        )
    for j in range(slots):
        at = j * block
        pieces.append(
            (own + prev + at, 0, kb_ref[at : at + block, :], vb_ref[at : at + block, :], count > j)
        )

    def pad_rows(x, start, fill):
        if start == 0:
            return x
        return jnp.concatenate([jnp.full((x.shape[0], start), fill, x.dtype), x], axis=1)

    scores = []
    row_max = None
    for _, start, keys, _, ok in pieces:
        s = nt(keys, q[start:, :])
        if ok is None:
            d = jnp.where(diag, s[:, :half], -1e30)
            s = d if s.shape[1] == half else jnp.concatenate([d, s[:, half:]], axis=1)
            top = jnp.max(s, axis=0, keepdims=True)
        else:
            top = jnp.max(s, axis=0, keepdims=True) + jnp.where(ok, 0.0, -1e30)
        top = pad_rows(top, start, -1e30)
        row_max = top if row_max is None else jnp.maximum(row_max, top)
        scores.append(s)
    shift = row_max * c
    weights = []
    total = None
    for (_, start, _, _, ok), s in zip(pieces, scores):
        m = shift[:, start:]
        if ok is not None:
            m = m + jnp.where(ok, 0.0, 1e30)
        w = jnp.exp2(s * c - m)
        part = pad_rows(jnp.sum(w, axis=0, keepdims=True), start, 0.0)
        total = part if total is None else total + part
        weights.append(w)
    inv = 1.0 / total
    out_t = None
    probs = []
    for (_, start, _, vals, _), w in zip(pieces, weights):
        p = (w * inv[:, start:]).astype(BF)
        probs.append(p)
        o = pad_rows(nn(vals.T, p), start, 0.0)
        out_t = o if out_t is None else out_t + o
    out = out_t.T.astype(BF)
    out_ref[...] = out
    delta = jnp.sum(out.astype(F32) * g.astype(F32), axis=1, keepdims=True).T
    r2 = inv * scale

    @pl.when(step == 0)
    def _():
        acc_k[...] = jnp.zeros_like(acc_k)
        acc_v[...] = jnp.zeros_like(acc_v)

    gq_t = None
    for (at, start, keys, vals, _), w, p in zip(pieces, weights, probs):
        n = keys.shape[0]
        dp = nt(vals, g[start:, :])
        ds = ((w * r2[:, start:]) * (dp - delta[:, start:])).astype(BF)
        acc_v[at : at + n, :] += nn(p, g[start:, :])
        acc_k[at : at + n, :] += nn(ds, q[start:, :])
        d = pad_rows(nn(keys.T, ds), start, 0.0)
        gq_t = d if gq_t is None else gq_t + d
    gq_ref[...] = gq_t.T.astype(BF)

    @pl.when(step == group - 1)
    def _():
        dko_ref[...] = acc_k[:own, :]
        dvo_ref[...] = acc_v[:own, :]
        dkp_ref[...] = acc_k[own : own + prev, :].astype(BF)
        dvp_ref[...] = acc_v[own : own + prev, :].astype(BF)
        dkb_ref[...] = acc_k[own + prev :, :].astype(BF)
        dvb_ref[...] = acc_v[own + prev :, :].astype(BF)


def attention(q, g, k, v, kp, vp, kb, vb, count, hi, prev_groups, slots):
    rows, q_cols = q.shape
    own, kv_cols = k.shape
    prev, beac = kp.shape[0], kb.shape[0]
    heads, kv_heads = q_cols // HD, kv_cols // HD
    group = heads // kv_heads
    half = own // 2
    per_q = pl.BlockSpec((rows, HD), lambda a, b, *_: (0, a * group + b))

    def per_kv(n):
        return pl.BlockSpec((n, HD), lambda a, b, *_: (0, a))

    keys = own + prev + beac
    return pl.pallas_call(
        functools.partial(attention_kernel, group, prev_groups, slots, half),
        grid_spec=pltpu.PrefetchScalarGridSpec(
            num_scalar_prefetch=2,
            grid=(kv_heads, group),
            in_specs=[per_q, per_q, per_kv(own), per_kv(own), per_kv(prev), per_kv(prev), per_kv(beac), per_kv(beac)],
            out_specs=[per_q, per_q, per_kv(own), per_kv(own), per_kv(prev), per_kv(prev), per_kv(beac), per_kv(beac)],
            scratch_shapes=[pltpu.VMEM((keys, HD), F32), pltpu.VMEM((keys, HD), F32)],
        ),
        out_shape=[
            jax.ShapeDtypeStruct(q.shape, BF),
            jax.ShapeDtypeStruct(q.shape, BF),
            jax.ShapeDtypeStruct(k.shape, F32),
            jax.ShapeDtypeStruct(k.shape, F32),
            jax.ShapeDtypeStruct(kp.shape, BF),
            jax.ShapeDtypeStruct(kp.shape, BF),
            jax.ShapeDtypeStruct(kb.shape, BF),
            jax.ShapeDtypeStruct(kb.shape, BF),
        ],
        compiler_params=pltpu.CompilerParams(vmem_limit_bytes=50 * 1024 * 1024),
        cost_estimate=pl.CostEstimate(
            flops=12 * heads * rows * keys * HD, bytes_accessed=4 * q.size * 2, transcendentals=heads * rows * keys
        ),
    )(count, hi, q, g, k, v, kp, vp, kb, vb)


def deliver_kernel(
    groups, owners, slots,
    row_ref, count_ref, out_ref, gq_ref, dko_ref, dvo_ref, dkp_ref, dvp_ref, dkb_ref, dvb_ref,
    tout_ref, tgq_ref, tgk_ref, tgv_ref, bk_ref, bv_ref,
    near, back, summed, part, send, got,
    near_s, near_r, back_s, back_r, tok_s, tok_r, tok_l, kv_s, kv_r, kv_l, own_s, own_r,
):
    mesh_id = pl.DeviceIdType.MESH
    me = lax.axis_index("ctx")
    t = lax.axis_index("tp")
    hi, lo = t // CORES, t % CORES
    other = 1 - lo
    sibling = {"tp": hi * CORES + other}
    rows = dko_ref.shape[0]
    tokens = tout_ref.shape[0]
    block, bw = bk_ref.shape

    barrier = pltpu.get_barrier_semaphore()
    pl.semaphore_signal(barrier, inc=1, device_id=sibling, device_id_type=mesh_id)
    for d in range(1, groups):
        pl.semaphore_signal(
            barrier, inc=1, device_id={"tp": lax.rem(hi + d, groups) * CORES + lo}, device_id_type=mesh_id
        )
    for d in range(1, owners):
        pl.semaphore_signal(
            barrier, inc=1, device_id={"ctx": lax.rem(me + d, owners)}, device_id_type=mesh_id
        )
    pl.semaphore_wait(barrier, 1 + (groups - 1) + (owners - 1))

    def remote(src, dst, s, r, to):
        return pltpu.make_async_remote_copy(
            src_ref=src, dst_ref=dst, send_sem=s, recv_sem=r, device_id=to, device_id_type=mesh_id
        )

    nears = []
    for d in range(1, groups):
        there = lax.rem(hi + d, groups)
        for x, ref in enumerate((dkb_ref, dvb_ref)):
            nears.append(
                remote(
                    ref.at[:, pl.ds(pl.multiple_of(there * bw, bw), bw)], near.at[d, x],
                    near_s.at[d, x], near_r.at[d, x], {"tp": there * CORES + lo},
                )
            )
    for cp in nears:
        cp.start()

    def back_copy(d, x):
        ref = (dkp_ref, dvp_ref)[x]
        return remote(
            ref.at[pl.ds((d - 1) * rows, rows)], back.at[d, x], back_s.at[d, x], back_r.at[d, x],
            {"tp": jnp.maximum(hi - d, 0) * CORES + lo},
        )

    for d in range(1, groups):

        @pl.when(hi >= d)
        def _(d=d):
            for x in range(2):
                back_copy(d, x).start()

    def swap(x, src, dst, s, r, l):
        width = src.shape[1] // groups
        res = []
        for j in range(groups):
            cols = pl.ds(pl.multiple_of((CORES * j + lo) * width, width), width)
            away = src.at[pl.ds(pl.multiple_of(other * tokens, tokens), tokens), pl.ds(j * width, width)]
            here = src.at[pl.ds(pl.multiple_of(lo * tokens, tokens), tokens), pl.ds(j * width, width)]
            res.append(
                (
                    remote(away, dst.at[:, cols], s.at[x, j], r.at[x, j], sibling),
                    pltpu.make_async_copy(here, dst.at[:, cols], l.at[x, j]),
                )
            )
        return res

    swaps = swap(0, out_ref, tout_ref, tok_s, tok_r, tok_l) + swap(1, gq_ref, tgq_ref, tok_s, tok_r, tok_l)
    for far, local in swaps:
        far.start()
        local.start()

    for cp in nears:
        cp.wait_recv()
    mine = pl.ds(pl.multiple_of(hi * bw, bw), bw)
    for x, ref in enumerate((dkb_ref, dvb_ref)):
        acc = ref[:, mine].astype(F32)
        for d in range(1, groups):
            acc = acc + near[d, x].astype(F32)
        part[x] = acc

    def own_copy(d):
        return remote(
            send.at[d], got.at[d], own_s.at[d], own_r.at[d], {"ctx": jnp.maximum(me - d, 0)}
        )

    for d in range(owners - 1, 0, -1):

        @pl.when(me >= d)
        def _(d=d):
            for x in range(2):
                acc = jnp.zeros((block, bw), F32)
                for j in range(slots):
                    hit = jnp.logical_and(row_ref[0, j] == me - d, count_ref[0] > j)
                    acc = acc + part[x, j * block : (j + 1) * block, :] * jnp.where(hit, 1.0, 0.0)
                send[d, x] = acc.astype(BF)
            own_copy(d).start()

    summed[0] = dko_ref[...].astype(BF)
    summed[1] = dvo_ref[...].astype(BF)
    for d in range(1, groups):

        @pl.when(hi + d < groups)
        def _(d=d):
            for x, ref in enumerate((dko_ref, dvo_ref)):
                back_copy(d, x).wait_recv()
                base = ref[...] if d == 1 else summed[x].astype(F32)
                summed[x] = (base + back[d, x].astype(F32)).astype(BF)

    kvs = swap(0, summed.at[0], tgk_ref, kv_s, kv_r, kv_l) + swap(1, summed.at[1], tgv_ref, kv_s, kv_r, kv_l)
    for far, local in kvs:
        far.start()
        local.start()

    part[:, :block, :] = jnp.zeros((2, block, bw), F32)
    for d in range(1, owners):

        @pl.when(me + d < owners)
        def _(d=d):
            own_copy(d).wait_recv()
            part[:, :block, :] += got[d].astype(F32)

    bk_ref[...] = part[0, :block, :].astype(BF)
    bv_ref[...] = part[1, :block, :].astype(BF)
    for far, local in swaps + kvs:
        far.wait_recv()
        far.wait_send()
        local.wait()
    for cp in nears:
        cp.wait_send()
    for d in range(1, groups):

        @pl.when(hi >= d)
        def _(d=d):
            for x in range(2):
                back_copy(d, x).wait_send()

    for d in range(1, owners):

        @pl.when(me >= d)
        def _(d=d):
            own_copy(d).wait_send()


def deliver(row, count, out, gq, dko, dvo, dkp, dvp, dkb, dvb, groups, owners, tokens, bw):
    slots = row.shape[1]
    block = dkb.shape[0] // slots
    rows, cols = dko.shape
    vm = pl.BlockSpec(memory_space=pltpu.VMEM)
    sm = pl.BlockSpec(memory_space=pltpu.SMEM)
    hbm = pl.BlockSpec(memory_space=pl.ANY)
    dma = pltpu.SemaphoreType.DMA
    tok_q = jax.ShapeDtypeStruct((tokens, out.shape[1] * CORES), BF)
    tok_k = jax.ShapeDtypeStruct((tokens, cols * CORES), BF)
    bea = jax.ShapeDtypeStruct((block, bw), BF)
    pair = dma((groups, 2))
    two = dma((2, groups))
    return pl.pallas_call(
        functools.partial(deliver_kernel, groups, owners, slots),
        out_shape=[tok_q, tok_q, tok_k, tok_k, bea, bea],
        in_specs=[sm, sm, hbm, hbm] + [vm] * 6,
        out_specs=[hbm, hbm, hbm, hbm, vm, vm],
        scratch_shapes=[
            pltpu.VMEM((groups, 2, slots * block, bw), BF),
            pltpu.VMEM((groups, 2, rows, cols), BF),
            pltpu.VMEM((2, rows, cols), BF),
            pltpu.VMEM((2, slots * block, bw), F32),
            pltpu.VMEM((owners, 2, block, bw), BF),
            pltpu.VMEM((owners, 2, block, bw), BF),
            pair, pair, pair, pair, two, two, two, two, two, two,
            dma((owners,)), dma((owners,)),
        ],
        compiler_params=pltpu.CompilerParams(
            collective_id=1, has_side_effects=True, vmem_limit_bytes=48 * 1024 * 1024
        ),
    )(row, count, out, gq, dko, dvo, dkp, dvp, dkb, dvb)


def shards(
    queries, keys_in, values_in, grad_output, beacon_keys, beacon_values, read_blocks, read_counts
):
    tp = lax.axis_size("tp")
    owners = lax.axis_size("ctx")
    groups = tp // CORES
    t = lax.axis_index("tp")
    hi, lo = t // CORES, t % CORES
    tokens = queries.shape[0]
    block_rows, bw = beacon_keys.shape
    slots = read_blocks.shape[1]
    row, count = read_blocks[0], read_counts[0]

    def column_half(x, which):
        w = x.shape[1] // tp
        parts = [
            lax.dynamic_slice_in_dim(x, (CORES * j + which) * w, w, axis=1) for j in range(groups)
        ]
        return jnp.concatenate(parts, axis=1)

    sibling = [(i, i ^ 1) for i in range(tp)]

    def by_rank(mine, theirs, axis):
        first = jnp.where(lo == 0, mine, theirs)
        second = jnp.where(lo == 0, theirs, mine)
        return jnp.concatenate([first, second], axis=axis)

    def swap_in(*arrays):
        widths = [a.shape[1] // CORES for a in arrays]
        send = jnp.concatenate([column_half(a, 1 - lo) for a in arrays], axis=1)
        got = lax.ppermute(send, "tp", sibling)
        res, at = [], 0
        for a, w in zip(arrays, widths):
            res.append(by_rank(column_half(a, lo), got[:, at : at + w], 0))
            at += w
        return res

    all_b = lax.all_gather(
        jnp.concatenate([beacon_keys, beacon_values], axis=1), "ctx", axis=0, tiled=True
    )
    k, v = swap_in(keys_in, values_in)
    kv = jnp.concatenate([k, v], axis=1)
    prevs = []
    for d in range(1, groups):
        pairs = [(i, i + CORES * d) for i in range(tp - CORES * d)]
        prevs.append(lax.ppermute(kv, "tp", pairs))
    kvp = jnp.concatenate(prevs, axis=0)
    half_cols = k.shape[1]
    q, g = swap_in(queries, grad_output)

    mine = jnp.concatenate(
        [lax.dynamic_slice_in_dim(all_b, row[j] * block_rows, block_rows, axis=0) for j in range(slots)],
        axis=0,
    )
    quarters = [mine]
    for d in range(1, groups):
        pairs = [(i, (i + CORES * d) % tp) for i in range(tp)]
        quarters.append(lax.ppermute(mine, "tp", pairs))
    def ordered(lo_col, hi_col):
        res = []
        for j in range(groups):
            x = quarters[0][:, lo_col:hi_col]
            for d in range(1, groups):
                x = jnp.where((hi - d) % groups == j, quarters[d][:, lo_col:hi_col], x)
            res.append(x)
        return jnp.concatenate(res, axis=1)

    kb, vb = ordered(0, bw), ordered(bw, 2 * bw)

    out, gq, dko, dvo, dkp, dvp, dkb, dvb = attention(
        q, g, k, v, kvp[:, :half_cols], kvp[:, half_cols:], kb, vb,
        count[None], hi[None].astype(jnp.int32), groups - 1, slots,
    )

    return tuple(
        deliver(
            read_blocks, read_counts, out, gq, dko, dvo, dkp, dvp, dkb, dvb, groups, owners, tokens, bw
        )
    )


def solution(mesh):
    tok = P(("ctx", "tp"), None)
    bea = P("ctx", "tp")
    return jax.shard_map(
        shards,
        mesh=mesh,
        in_specs=(tok, tok, tok, tok, bea, bea, P("ctx", None), P("ctx")),
        out_specs=(tok, tok, tok, tok, bea, bea),
        check_vma=False,
    )
```

```python
import functools
import math

import jax
import jax.numpy as jnp
from jax import lax
from jax.experimental import pallas as pl
from jax.experimental.pallas import tpu as pltpu
from jax.sharding import PartitionSpec as P

HD = 128
CORES = 2
BF = jnp.bfloat16
F32 = jnp.float32


def nt(a, b):
    return lax.dot_general(a, b, (((1,), (1,)), ((), ())), preferred_element_type=F32)


def nn(a, b):
    return jnp.dot(a, b, preferred_element_type=F32)


def attention_kernel(
    group, prev_groups, slots, half,
    count_ref, hi_ref,
    q_ref, g_ref, k_ref, v_ref, kp_ref, vp_ref, kb_ref, vb_ref,
    out_ref, gq_ref, dko_ref, dvo_ref, dkp_ref, dvp_ref, dkb_ref, dvb_ref,
    acc_k, acc_v,
):
    step = pl.program_id(1)
    rows = q_ref.shape[0]
    own = k_ref.shape[0]
    prev = kp_ref.shape[0]
    beac = kb_ref.shape[0]
    chunk = prev // prev_groups
    block = beac // slots
    scale = HD ** (-0.5)
    c = scale * math.log2(math.e)
    q = q_ref[...]
    g = g_ref[...]
    hi = hi_ref[0]
    count = count_ref[0]

    diag = lax.broadcasted_iota(jnp.int32, (half, half), 0) <= lax.broadcasted_iota(
        jnp.int32, (half, half), 1
    )
    pieces = []
    for i in range(0, own, half):
        pieces.append((i, i, k_ref[i : i + half, :], v_ref[i : i + half, :], None))
    for d in range(prev_groups):
        at = d * chunk
        pieces.append(
            (own + at, 0, kp_ref[at : at + chunk, :], vp_ref[at : at + chunk, :], hi > d)
        )
    for j in range(slots):
        at = j * block
        pieces.append(
            (own + prev + at, 0, kb_ref[at : at + block, :], vb_ref[at : at + block, :], count > j)
        )

    def pad_rows(x, start, fill):
        if start == 0:
            return x
        return jnp.concatenate([jnp.full((x.shape[0], start), fill, x.dtype), x], axis=1)

    scores = []
    row_max = None
    for _, start, keys, _, ok in pieces:
        s = nt(keys, q[start:, :])
        if ok is None:
            d = jnp.where(diag, s[:, :half], -1e30)
            s = d if s.shape[1] == half else jnp.concatenate([d, s[:, half:]], axis=1)
            top = jnp.max(s, axis=0, keepdims=True)
        else:
            top = jnp.max(s, axis=0, keepdims=True) + jnp.where(ok, 0.0, -1e30)
        top = pad_rows(top, start, -1e30)
        row_max = top if row_max is None else jnp.maximum(row_max, top)
        scores.append(s)
    shift = row_max * c
    weights = []
    total = None
    for (_, start, _, _, ok), s in zip(pieces, scores):
        m = shift[:, start:]
        if ok is not None:
            m = m + jnp.where(ok, 0.0, 1e30)
        w = jnp.exp2(s * c - m)
        part = pad_rows(jnp.sum(w, axis=0, keepdims=True), start, 0.0)
        total = part if total is None else total + part
        weights.append(w)
    inv = 1.0 / total
    out_t = None
    probs = []
    for (_, start, _, vals, _), w in zip(pieces, weights):
        p = (w * inv[:, start:]).astype(BF)
        probs.append(p)
        o = pad_rows(nn(vals.T, p), start, 0.0)
        out_t = o if out_t is None else out_t + o
    out = out_t.T.astype(BF)
    out_ref[...] = out
    delta = jnp.sum(out.astype(F32) * g.astype(F32), axis=1, keepdims=True).T
    r2 = inv * scale

    @pl.when(step == 0)
    def _():
        acc_k[...] = jnp.zeros_like(acc_k)
        acc_v[...] = jnp.zeros_like(acc_v)

    gq_t = None
    for (at, start, keys, vals, _), w, p in zip(pieces, weights, probs):
        n = keys.shape[0]
        dp = nt(vals, g[start:, :])
        ds = ((w * r2[:, start:]) * (dp - delta[:, start:])).astype(BF)
        acc_v[at : at + n, :] += nn(p, g[start:, :])
        acc_k[at : at + n, :] += nn(ds, q[start:, :])
        d = pad_rows(nn(keys.T, ds), start, 0.0)
        gq_t = d if gq_t is None else gq_t + d
    gq_ref[...] = gq_t.T.astype(BF)

    @pl.when(step == group - 1)
    def _():
        dko_ref[...] = acc_k[:own, :]
        dvo_ref[...] = acc_v[:own, :]
        dkp_ref[...] = acc_k[own : own + prev, :].astype(BF)
        dvp_ref[...] = acc_v[own : own + prev, :].astype(BF)
        dkb_ref[...] = acc_k[own + prev :, :].astype(BF)
        dvb_ref[...] = acc_v[own + prev :, :].astype(BF)


def attention(q, g, k, v, kp, vp, kb, vb, count, hi, prev_groups, slots):
    rows, q_cols = q.shape
    own, kv_cols = k.shape
    prev, beac = kp.shape[0], kb.shape[0]
    heads, kv_heads = q_cols // HD, kv_cols // HD
    group = heads // kv_heads
    half = own // 2
    per_q = pl.BlockSpec((rows, HD), lambda a, b, *_: (0, a * group + b))

    def per_kv(n):
        return pl.BlockSpec((n, HD), lambda a, b, *_: (0, a))

    keys = own + prev + beac
    return pl.pallas_call(
        functools.partial(attention_kernel, group, prev_groups, slots, half),
        grid_spec=pltpu.PrefetchScalarGridSpec(
            num_scalar_prefetch=2,
            grid=(kv_heads, group),
            in_specs=[per_q, per_q, per_kv(own), per_kv(own), per_kv(prev), per_kv(prev), per_kv(beac), per_kv(beac)],
            out_specs=[per_q, per_q, per_kv(own), per_kv(own), per_kv(prev), per_kv(prev), per_kv(beac), per_kv(beac)],
            scratch_shapes=[pltpu.VMEM((keys, HD), F32), pltpu.VMEM((keys, HD), F32)],
        ),
        out_shape=[
            jax.ShapeDtypeStruct(q.shape, BF),
            jax.ShapeDtypeStruct(q.shape, BF),
            jax.ShapeDtypeStruct(k.shape, F32),
            jax.ShapeDtypeStruct(k.shape, F32),
            jax.ShapeDtypeStruct(kp.shape, BF),
            jax.ShapeDtypeStruct(kp.shape, BF),
            jax.ShapeDtypeStruct(kb.shape, BF),
            jax.ShapeDtypeStruct(kb.shape, BF),
        ],
        compiler_params=pltpu.CompilerParams(vmem_limit_bytes=50 * 1024 * 1024),
        cost_estimate=pl.CostEstimate(
            flops=12 * heads * rows * keys * HD, bytes_accessed=4 * q.size * 2, transcendentals=heads * rows * keys
        ),
    )(count, hi, q, g, k, v, kp, vp, kb, vb)


def owners_kernel(dense_ref, out_ref, got, total, send_sem, recv_sem):
    me = lax.axis_index("ctx")
    n = got.shape[0]
    block = got.shape[1]
    barrier = pltpu.get_barrier_semaphore()
    for d in range(1, n):
        pl.semaphore_signal(
            barrier, inc=1, device_id={"ctx": lax.rem(me + d, n)}, device_id_type=pl.DeviceIdType.MESH
        )
    pl.semaphore_wait(barrier, n - 1)

    def copy(d):
        to = jnp.maximum(me - d, 0)
        return pltpu.make_async_remote_copy(
            src_ref=dense_ref.at[pl.ds(pl.multiple_of(to * block, block), block)],
            dst_ref=got.at[d],
            send_sem=send_sem.at[d],
            recv_sem=recv_sem.at[d],
            device_id={"ctx": to},
            device_id_type=pl.DeviceIdType.MESH,
        )

    for d in range(n - 1, 0, -1):

        @pl.when(me >= d)
        def _(d=d):
            copy(d).start()

    total[...] = jnp.zeros_like(total)
    for d in range(1, n):

        @pl.when(me + d < n)
        def _(d=d):
            copy(d).wait_recv()
            total[...] += got[d].astype(F32)

    out_ref[...] = total[...].astype(BF)
    for d in range(1, n):

        @pl.when(me >= d)
        def _(d=d):
            copy(d).wait_send()


def to_owners(dense, owners):
    block, width = dense.shape[0] // owners, dense.shape[1]
    return pl.pallas_call(
        owners_kernel,
        out_shape=jax.ShapeDtypeStruct((block, width), BF),
        in_specs=[pl.BlockSpec(memory_space=pltpu.VMEM)],
        out_specs=pl.BlockSpec(memory_space=pltpu.VMEM),
        scratch_shapes=[
            pltpu.VMEM((owners, block, width), BF),
            pltpu.VMEM((block, width), F32),
            pltpu.SemaphoreType.DMA((owners,)),
            pltpu.SemaphoreType.DMA((owners,)),
        ],
        compiler_params=pltpu.CompilerParams(
            collective_id=1, has_side_effects=True, vmem_limit_bytes=32 * 1024 * 1024
        ),
        cost_estimate=pl.CostEstimate(
            flops=dense.size, bytes_accessed=2 * owners * dense.size * 2, transcendentals=0
        ),
    )(dense)


def shards(
    queries, keys_in, values_in, grad_output, beacon_keys, beacon_values, read_blocks, read_counts
):
    tp = lax.axis_size("tp")
    owners = lax.axis_size("ctx")
    groups = tp // CORES
    t = lax.axis_index("tp")
    hi, lo = t // CORES, t % CORES
    tokens = queries.shape[0]
    block_rows, bw = beacon_keys.shape
    slots = read_blocks.shape[1]
    row, count = read_blocks[0], read_counts[0]

    def column_half(x, which):
        w = x.shape[1] // tp
        parts = [
            lax.dynamic_slice_in_dim(x, (CORES * j + which) * w, w, axis=1) for j in range(groups)
        ]
        return jnp.concatenate(parts, axis=1)

    sibling = [(i, i ^ 1) for i in range(tp)]

    def by_rank(mine, theirs, axis):
        first = jnp.where(lo == 0, mine, theirs)
        second = jnp.where(lo == 0, theirs, mine)
        return jnp.concatenate([first, second], axis=axis)

    def swap_in(*arrays):
        widths = [a.shape[1] // CORES for a in arrays]
        send = jnp.concatenate([column_half(a, 1 - lo) for a in arrays], axis=1)
        got = lax.ppermute(send, "tp", sibling)
        res, at = [], 0
        for a, w in zip(arrays, widths):
            res.append(by_rank(column_half(a, lo), got[:, at : at + w], 0))
            at += w
        return res

    all_b = lax.all_gather(
        jnp.concatenate([beacon_keys, beacon_values], axis=1), "ctx", axis=0, tiled=True
    )
    k, v = swap_in(keys_in, values_in)
    kv = jnp.concatenate([k, v], axis=1)
    prevs = []
    for d in range(1, groups):
        pairs = [(i, i + CORES * d) for i in range(tp - CORES * d)]
        prevs.append(lax.ppermute(kv, "tp", pairs))
    kvp = jnp.concatenate(prevs, axis=0)
    half_cols = k.shape[1]
    q, g = swap_in(queries, grad_output)

    mine = jnp.concatenate(
        [lax.dynamic_slice_in_dim(all_b, row[j] * block_rows, block_rows, axis=0) for j in range(slots)],
        axis=0,
    )
    quarters = [mine]
    for d in range(1, groups):
        pairs = [(i, (i + CORES * d) % tp) for i in range(tp)]
        quarters.append(lax.ppermute(mine, "tp", pairs))
    def ordered(lo_col, hi_col):
        res = []
        for j in range(groups):
            x = quarters[0][:, lo_col:hi_col]
            for d in range(1, groups):
                x = jnp.where((hi - d) % groups == j, quarters[d][:, lo_col:hi_col], x)
            res.append(x)
        return jnp.concatenate(res, axis=1)

    kb, vb = ordered(0, bw), ordered(bw, 2 * bw)

    out, gq, dko, dvo, dkp, dvp, dkb, dvb = attention(
        q, g, k, v, kvp[:, :half_cols], kvp[:, half_cols:], kb, vb,
        count[None], hi[None].astype(jnp.int32), groups - 1, slots,
    )

    def quarter(x, j):
        return lax.dynamic_slice_in_dim(x, j * bw, bw, axis=1)

    def both(j):
        return jnp.concatenate([quarter(dkb, j), quarter(dvb, j)], axis=1)

    beacon = both(hi).astype(F32)
    back = jnp.concatenate([dkp, dvp], axis=1)
    for d in range(1, groups):
        pairs = [(i, (i + CORES * d) % tp) for i in range(tp)]
        there = lax.ppermute(both((hi + d) % groups), "tp", pairs)
        back, there = lax.optimization_barrier((back, there))
        beacon = beacon + there.astype(F32)
    beacon = beacon.reshape(slots, block_rows, 2 * bw)
    used = jnp.arange(slots, dtype=jnp.int32) < count
    ids = jnp.arange(owners, dtype=jnp.int32)
    dense = jnp.zeros((owners, block_rows, 2 * bw), F32)
    for j in range(slots):
        hit = (ids == row[j]) & used[j]
        dense = dense + jnp.where(hit[:, None, None], beacon[j][None], 0.0)
    dense = dense.astype(BF).reshape(owners * block_rows, 2 * bw)
    own_b = to_owners(dense, owners)

    rows_g = k.shape[0]
    kvg = jnp.concatenate([dko, dvo], axis=1)
    for d in range(1, groups):
        pairs = [(i + CORES * d, i) for i in range(tp - CORES * d)]
        term = lax.ppermute(back[(d - 1) * rows_g : d * rows_g], "tp", pairs)
        term, own_b = lax.optimization_barrier((term, own_b))
        kvg = kvg + term.astype(F32)
    kvg = kvg.astype(BF)

    def swap_out(*arrays):
        send = jnp.concatenate(
            [lax.dynamic_slice_in_dim(a, (1 - lo) * tokens, tokens, axis=0) for a in arrays], axis=1
        )
        got = lax.ppermute(send, "tp", sibling)
        res, at = [], 0
        for a in arrays:
            n = a.shape[1]
            keep = lax.dynamic_slice_in_dim(a, lo * tokens, tokens, axis=0)
            new = got[:, at : at + n]
            at += n
            w = n // groups
            cols = []
            for j in range(groups):
                cols.append(by_rank(keep[:, j * w : (j + 1) * w], new[:, j * w : (j + 1) * w], 1))
            res.append(jnp.concatenate(cols, axis=1))
        return res

    tok_out, tok_gq = swap_out(out, gq)
    tok_gk, tok_gv = swap_out(kvg[:, :half_cols], kvg[:, half_cols:])
    return (tok_out, tok_gq, tok_gk, tok_gv, own_b[:, :bw], own_b[:, bw:])


def solution(mesh):
    tok = P(("ctx", "tp"), None)
    bea = P("ctx", "tp")
    return jax.shard_map(
        shards,
        mesh=mesh,
        in_specs=(tok, tok, tok, tok, bea, bea, P("ctx", None), P("ctx")),
        out_specs=(tok, tok, tok, tok, bea, bea),
        check_vma=False,
    )
```
